32 devices in a mesh: dom: 2 (over x), gy: 4 (over y, core), gz: 4 (over z).
Axes of the slice: x: 2, y: 2, z: 4, core: 2. Of those that a mesh axis runs over, the one named last changes fastest.
Arguments:
- right_side: float32 [32, 256, 512], P('dom', 'gy', 'gz'), may hold values from -8 to 8
- coefficient: float32 [32, 256, 512], P('dom', 'gy', 'gz'), may hold values from 0.1 to 10
Outputs:
- solution: float32 [32, 256, 512], P('dom', 'gy', 'gz')
- residual: float32 [32, 256, 512], P('dom', 'gy', 'gz')
The draws below stay inside these ranges and needn't reach their ends.
All inputs are finite; a program needn't handle non-finite values.
Results may differ from the reference program's by a relative error of at most 0.00028.
Values sent between devices are 32-bit elements; how exact they have to be, the bound alone decides.
A program may use at most 128 MiB of HBM per device.

```python
import math
import jax
import jax.numpy as jnp

LEVELS = 4
NU = 2
COARSE_SWEEPS = 8
NX = 32
NY = 256
NZ = 512


def block_levels(rng, shape, split, least, top_value):
    level = 1.0
    for dim, blocks in split:
        steps = jax.random.uniform(jax.random.fold_in(jax.random.fold_in(rng, 6), dim), (blocks,), jnp.float32, least / len(split), top_value / len(split))
        level = level * jnp.repeat(jnp.exp(steps), shape[dim] // blocks).reshape((-1,) + (1,) * (len(shape) - 1 - dim))
    return level


def centred(own_key, dims, spread, most, pieces=(), kind=jnp.bfloat16):
    values = jax.random.normal(own_key, dims, jnp.float32) * spread
    if len(pieces) > 0:
        values = block_levels(own_key, dims, pieces, -0.22, 0.18) * values
    return jnp.clip(values, min=-most, max=most).astype(kind)


def setup_inputs(seed: int = 0) -> dict:
    keys = jax.random.split(jax.random.key(seed), 3)
    return {
        "right_side": centred(keys[0], (NX, NY, NZ), 1.0, 8.0, ((0, 2), (1, 4), (2, 4)), jnp.float32),
        "coefficient": jnp.clip(jnp.exp(math.log(10.0) - 4.6051702 * jax.random.uniform(keys[1], (NX, NY, NZ), jnp.float32) ** block_levels(keys[1], (NX, NY, NZ), ((0, 2), (1, 4), (2, 4)), -0.2, 0.2)), 0.1, 10.0),
    }


OMEGA = 0.8


def neighbours(padded):
    return (padded[2:, 1:-1, 1:-1], padded[:-2, 1:-1, 1:-1], padded[1:-1, 2:, 1:-1],
            padded[1:-1, :-2, 1:-1], padded[1:-1, 1:-1, 2:], padded[1:-1, 1:-1, :-2])


def face_weights(coefficient):
    result = []
    for beside in neighbours(jnp.pad(coefficient, 1)):
        result.append(0.5 * (coefficient + beside))
    summed = result[0]
    for weight in result[1:]:
        summed = summed + weight
    return tuple(result), summed


def apply_operator(iterate, weights):
    summed = jnp.zeros_like(iterate)
    for weight, beside in zip(weights, neighbours(jnp.pad(iterate, 1))):
        summed = summed + weight * (iterate - beside)
    return summed


def smooth(iterate, source, weights, diagonal, sweeps):
    for sweep_index in range(sweeps):
        iterate = iterate + OMEGA * (source - apply_operator(iterate, weights)) / diagonal
    return iterate


def coarsen_sum(values):
    size_x, size_y, size_z = values.shape
    return values.reshape(size_x // 2, 2, size_y // 2, 2, size_z // 2, 2).sum(axis=(1, 3, 5))


def prolong(values):
    return jnp.repeat(jnp.repeat(jnp.repeat(values, 2, 0), 2, 1), 2, 2)


def reference(right_side, coefficient):
    sources = [right_side]
    coefficients = [coefficient]
    operators = []
    smoothed = []
    for level_index in range(LEVELS):
        weights, diagonal = face_weights(coefficients[-1])
        operators.append((weights, diagonal))
        iterate = smooth(jnp.zeros_like(sources[-1]), sources[-1], weights, diagonal, NU)
        smoothed.append(iterate)
        remainder = sources[-1] - apply_operator(iterate, weights)
        sources.append(0.5 * coarsen_sum(remainder))
        coefficients.append(0.125 * coarsen_sum(coefficients[-1]))
    weights, diagonal = face_weights(coefficients[-1])
    correction = smooth(jnp.zeros_like(sources[-1]), sources[-1], weights, diagonal, COARSE_SWEEPS)
    for level_index in range(LEVELS - 1, -1, -1):
        weights, diagonal = operators[level_index]
        iterate = smoothed[level_index] + prolong(correction)
        correction = smooth(iterate, sources[level_index], weights, diagonal, NU)
    solution = correction
    residual = right_side - apply_operator(solution, operators[0][0])
    return solution, residual
```

```python
import functools
import jax
import jax.numpy as jnp
from jax import lax
from jax.experimental import pallas as pl
from jax.experimental.pallas import tpu as pltpu
from jax.sharding import PartitionSpec as P

NU = 2
COARSE_SWEEPS = 8
OMEGA = 0.8
LANES = 128
PAD = 8
AXES = ("dom", "gy", "gz")
MESH = pl.DeviceIdType.MESH
F32 = jnp.float32
HI = lax.Precision.HIGHEST
UNROLL = 2


def loop(n, body, init=None, unroll=UNROLL):
    unroll = min(unroll, n)
    if init is None:
        lax.fori_loop(0, n, lambda i, c: (body(i), c)[1], 0, unroll=unroll)
        return None
    return lax.fori_loop(0, n, body, init, unroll=unroll)


def lane_index(rows):
    return lax.broadcasted_iota(jnp.int32, (rows, LANES), 1)


def pair_sum_matrix(nz):
    row = lax.broadcasted_iota(jnp.int32, (LANES, LANES), 0)
    col = lax.broadcasted_iota(jnp.int32, (LANES, LANES), 1)
    return jnp.where((row // 2 == col) & (row < nz), 1.0, 0.0).astype(F32)


def pair_copy_matrix(nz):
    row = lax.broadcasted_iota(jnp.int32, (LANES, LANES), 0)
    col = lax.broadcasted_iota(jnp.int32, (LANES, LANES), 1)
    return jnp.where((col // 2 == row) & (col < nz), 1.0, 0.0).astype(F32)


class Plan:
    def __init__(self, sizes, local):
        self.sizes = sizes
        self.names = []
        self.shapes = []
        nx, ny, nz = local
        self.local = local
        self.dims = {0: (nx, ny, nz), 1: (nx // 2, ny // 2, nz // 2)}
        self.piece = (nx // 4, ny // 4, nz // 4)
        for level in (2, 3, 4):
            s = 2**level
            self.dims[level] = tuple(d * n // s for d, n in zip(sizes, local))
        assert self.dims[2][2] <= LANES and self.piece[0] * self.piece[2] <= LANES
        self.rounds = 0
        for level in range(5):
            x, y, z = self.dims[level]
            fields = {0: "KABCDE", 1: "KABCDE", 2: "KABCDE", 3: "KABCDE", 4: "KAB"}[level]
            for field in fields:
                self.add("v%d%s" % (level, field), (x + 2, y + 2 * PAD, LANES))
            self.add("w%d" % level, (6, x, y, LANES))
            for field in "dqg":
                self.add("%s%d" % (field, level), (x, y, LANES))
            if level < 4:
                self.add("t%d" % level, (x // 2, y, LANES))
            if level < 2:
                for field in "KABCDE":
                    self.add("zs%d%s" % (level, field), (2, y, LANES))
                    self.add("zr%d%s" % (level, field), (2, y, LANES))
        for field in "KF":
            self.add("gb" + field, tuple(sizes) + (self.piece[1], LANES))
        self.sem_base = len(self.shapes)
        self.exchanges = {(l, c): i for i, (l, c) in enumerate(
            [(0, "K"), (1, "K"), (0, "A"), (0, "B"), (1, "A"), (1, "B"),
             (1, "C"), (1, "D"), (0, "C"), (0, "D"), (0, "E")])}
        n = len(self.exchanges)
        peers = max(sizes)
        self.names += ["es", "er", "gs", "gr"]
        self.shapes += [pltpu.SemaphoreType.DMA((n, 6)), pltpu.SemaphoreType.DMA((n, 6)),
                        pltpu.SemaphoreType.DMA((6, peers)), pltpu.SemaphoreType.DMA((6, peers))]

    def add(self, name, shape):
        self.names.append(name)
        self.shapes.append(pltpu.VMEM(shape, F32))


def kernel(plan, f_ref, k_ref, sol_ref, res_ref, *scratch):
    ref = dict(zip(plan.names, scratch))
    sizes = plan.sizes
    me = [lax.axis_index(a) for a in AXES]

    def copies(level, field):
        x, y, z = plan.dims[level]
        v = ref["v%d%s" % (level, field)]
        zs, zr = ref["zs%d%s" % (level, field)], ref["zr%d%s" % (level, field)]
        rnd = plan.exchanges[(level, field)]
        rows, planes = pl.ds(PAD, y), pl.ds(1, x)
        ends = [
            (v.at[x, rows], v.at[0, rows]), (v.at[1, rows], v.at[x + 1, rows]),
            (v.at[planes, pl.ds(PAD + y - 1, 1)], v.at[planes, pl.ds(PAD - 1, 1)]),
            (v.at[planes, pl.ds(PAD, 1)], v.at[planes, pl.ds(PAD + y, 1)]),
            (zs.at[1], zr.at[0]), (zs.at[0], zr.at[1]),
        ]
        result = []
        for i, (src, dst) in enumerate(ends):
            axis, up = i // 2, i % 2 == 0
            n, at = sizes[axis], me[axis]
            to = lax.rem(at + 1, n) if up else lax.rem(at + n - 1, n)
            copy = pltpu.make_async_remote_copy(
                src_ref=src, dst_ref=dst, send_sem=ref["es"].at[rnd, i], recv_sem=ref["er"].at[rnd, i],
                device_id={AXES[axis]: to}, device_id_type=MESH)
            sends = at < n - 1 if up else at > 0
            gets = at > 0 if up else at < n - 1
            result.append((copy, sends, gets))
        return result

    def start(level, field):
        for copy, sends, _ in copies(level, field):
            pl.when(sends)(copy.start)

    def finish(level, field):
        for copy, _, gets in copies(level, field):
            pl.when(gets)(copy.wait_recv)

    def drain(level, field):
        for copy, sends, _ in copies(level, field):
            pl.when(sends)(copy.wait_send)

    def zero_edges(level, field):
        x, y, z = plan.dims[level]
        v = ref["v%d%s" % (level, field)]
        zr = ref["zr%d%s" % (level, field)]
        spots = [v.at[0], v.at[x + 1], v.at[pl.ds(0, x + 2), pl.ds(0, PAD)],
                 v.at[pl.ds(0, x + 2), pl.ds(PAD + y, PAD)], zr.at[0], zr.at[1]]
        for i, spot in enumerate(spots):
            edge = me[i // 2] == (0 if i % 2 == 0 else sizes[i // 2] - 1)

            @pl.when(edge)
            def _():
                spot[...] = jnp.zeros(spot.shape, F32)

    def gather_copies(field, stage):
        gb = ref["gb" + field]
        axis = 2 - stage
        n, at = sizes[axis], me[axis]
        base = (0 if field == "K" else 3) + stage
        result = []
        for s in range(1, n):
            to, frm = lax.rem(at + s, n), lax.rem(at + n - s, n)
            index = tuple(me[: axis + 1])
            other = tuple(me[:axis]) + (frm,)
            make = functools.partial(
                pltpu.make_async_remote_copy, send_sem=ref["gs"].at[base, s], recv_sem=ref["gr"].at[base, s],
                device_id={AXES[axis]: to}, device_id_type=MESH)
            result.append((make(src_ref=gb.at[index], dst_ref=gb.at[index]),
                           make(src_ref=gb.at[other], dst_ref=gb.at[other])))
        return result

    def gather_start(field, stage):
        for out, _ in gather_copies(field, stage):
            out.start()

    def gather_finish(field, stage):
        for _, into in gather_copies(field, stage):
            into.wait_recv()

    def gather_drain(field, stage):
        for out, _ in gather_copies(field, stage):
            out.wait_send()

    def shifted(level, field, i):
        x, y, z = plan.dims[level]
        v = ref["v%d%s" % (level, field)]
        lane = lane_index(y)
        mid = v[i + 1, pl.ds(PAD, y), :]
        zp = pltpu.roll(mid, LANES - 1, 1)
        zm = pltpu.roll(mid, 1, 1)
        if level < 2:
            zr = ref["zr%d%s" % (level, field)]
            zp = jnp.where(lane == z - 1, pltpu.roll(zr[1], lax.rem(LANES + z - 1 - i, LANES), 1), zp)
            zm = jnp.where(lane == 0, pltpu.roll(zr[0], lax.rem(LANES - i, LANES), 1), zm)
        return mid, (v[i + 2, pl.ds(PAD, y), :], v[i, pl.ds(PAD, y), :],
                     v[i + 1, pl.ds(PAD + 1, y), :], v[i + 1, pl.ds(PAD - 1, y), :], zp, zm)

    def total(level, field, i):
        w = ref["w%d" % level]
        mid, beside = shifted(level, field, i)
        parts = [w[j, i] * b for j, b in enumerate(beside)]
        g = ref["g%d" % level][i]
        return mid, ((parts[0] + parts[1]) + (parts[2] + parts[3])) + ((parts[4] + parts[5]) + g)

    def fill(level, field, plane):
        x, y, z = plan.dims[level]
        v = ref["v%d%s" % (level, field)]
        if level < 2 and (level, field) in plan.exchanges:
            lane = lane_index(y)

            def body(i, carry):
                low, high = carry
                value = plane(i)
                v[i + 1, pl.ds(PAD, y), :] = value
                low = jnp.where(lane == i, jnp.broadcast_to(value[:, 0:1], (y, LANES)), low)
                high = jnp.where(lane == i, jnp.broadcast_to(value[:, z - 1:z], (y, LANES)), high)
                return low, high

            zero = jnp.zeros((y, LANES), F32)
            low, high = loop(x, body, (zero, zero))
            zs = ref["zs%d%s" % (level, field)]
            zs[0] = low
            zs[1] = high
        else:
            def body(i):
                v[i + 1, pl.ds(PAD, y), :] = plane(i)

            loop(x, body)

    def sweep(level, src, dst):
        def plane(i):
            mid, t = total(level, src, i)
            return (1.0 - OMEGA) * mid + t

        fill(level, dst, plane)

    def prepare(level):
        x, y, z = plan.dims[level]
        lane = lane_index(y)
        inside = lane < z
        w, d, q = ref["w%d" % level], ref["d%d" % level], ref["q%d" % level]

        def body(i):
            mid, beside = shifted(level, "K", i)
            beside = list(beside)
            if level >= 2:
                beside[4] = jnp.where(lane == z - 1, 0.0, beside[4])
                beside[5] = jnp.where(lane == 0, 0.0, beside[5])
            faces = [0.5 * (mid + b) for b in beside]
            diag = ((faces[0] + faces[1]) + (faces[2] + faces[3])) + (faces[4] + faces[5])
            scale = jnp.where(inside, OMEGA / jnp.where(inside, diag, 1.0), 0.0)
            d[i] = diag * (1.0 / OMEGA)
            q[i] = scale
            for j, face in enumerate(faces):
                weight = face * scale
                if level >= 2 and j == 4:
                    weight = jnp.where(lane == z - 1, 0.0, weight)
                if level >= 2 and j == 5:
                    weight = jnp.where(lane == 0, 0.0, weight)
                w[j, i] = weight

        loop(x, body)

    def restrict(level, plane, factor, store):
        x, y, z = plan.dims[level]
        t = ref["t%d" % level]
        matrix = pair_sum_matrix(z)

        def body(i):
            t[i] = plane(2 * i) + plane(2 * i + 1)

        loop(x // 2, body)

        def second(i):
            rows = t[i, pl.ds(0, y // 2, stride=2), :] + t[i, pl.ds(1, y // 2, stride=2), :]
            store(i, jnp.dot(rows * factor, matrix, precision=HI, preferred_element_type=F32))

        loop(x // 2, second)

    def residual(level, field):
        d = ref["d%d" % level]

        def plane(i):
            mid, t = total(level, field, i)
            return d[i] * (t - OMEGA * mid)

        return plane

    def correct(level, coarse):
        x, y, z = plan.dims[level]
        t = ref["t%d" % level]
        matrix = pair_copy_matrix(z)

        def body(i):
            rows = jnp.dot(coarse(i), matrix, precision=HI, preferred_element_type=F32)
            t[i, pl.ds(0, y // 2, stride=2), :] = rows
            t[i, pl.ds(1, y // 2, stride=2), :] = rows

        loop(x // 2, body)
        vb = ref["v%dB" % level]
        fill(level, "C", lambda i: vb[i + 1, pl.ds(PAD, y), :] + t[i // 2])

    px, py, pz = plan.piece

    def pack(pieces):
        whole = pieces[0]
        for i in range(1, px):
            whole = whole + pltpu.roll(pieces[i], i * pz, 1)
        return whole

    def unpack(field, store):
        gb = ref["gb" + field]
        lane = lane_index(py)
        for a in range(sizes[0]):
            for b in range(sizes[1]):
                for i in range(px):
                    rows = jnp.zeros((py, LANES), F32)
                    for c in range(sizes[2]):
                        part = gb[a, b, c]
                        shift = (pz * (c - i)) % LANES
                        if shift:
                            part = pltpu.roll(part, shift, 1)
                        rows = jnp.where(lane // pz == c, part, rows)
                    store(a * px + i, b * py, rows)

    def interior(level, field):
        x, y, z = plan.dims[level]
        v = ref["v%d%s" % (level, field)]

        def store(i, rows):
            v[i + 1, pl.ds(PAD, y), :] = rows

        return store

    def source(level):
        x, y, z = plan.dims[level]
        g, q = ref["g%d" % level], ref["q%d" % level]

        def store(i, rows):
            g[i] = q[i] * rows

        return store

    for level, field in plan.exchanges:
        zero_edges(level, field)
    barrier = pltpu.get_barrier_semaphore()
    for axis in range(3):
        for s in range(1, sizes[axis]):
            pl.semaphore_signal(barrier, inc=1, device_id={AXES[axis]: lax.rem(me[axis] + s, sizes[axis])},
                                device_id_type=MESH)

    k_plane = lambda i: k_ref[i]
    fill(0, "K", k_plane)
    restrict(0, k_plane, 0.125, interior(1, "K"))
    k1 = ref["v1K"]
    y1 = plan.dims[1][1]
    k1_plane = lambda i: k1[i + 1, pl.ds(PAD, y1), :]
    fill(1, "K", k1_plane)

    pl.semaphore_wait(barrier, sum(sizes) - 3)
    start(0, "K")
    start(1, "K")

    def own_piece(level_plane, factor, field):
        t = ref["t0"]

        def store(i, rows):
            t[i, pl.ds(0, py), :] = rows

        restrict(1, level_plane, factor, store)
        ref["gb" + field][me[0], me[1], me[2]] = pack([t[i, pl.ds(0, py), :] for i in range(px)])

    own_piece(k1_plane, 0.125, "K")
    gather_start("K", 0)
    for level in (2, 3, 4):
        x, y, z = plan.dims[level]
        for field in ("KAB" if level == 4 else "KABCDE"):
            v = ref["v%d%s" % (level, field)]
            v[0] = jnp.zeros(v.shape[1:], F32)
            v[x + 1] = jnp.zeros(v.shape[1:], F32)
            v[:, pl.ds(0, PAD), :] = jnp.zeros((x + 2, PAD, LANES), F32)
            v[:, pl.ds(PAD + y, PAD), :] = jnp.zeros((x + 2, PAD, LANES), F32)

    finish(0, "K")
    prepare(0)
    g0, q0 = ref["g0"], ref["q0"]

    def first(i):
        value = q0[i] * f_ref[i]
        g0[i] = value
        return value

    fill(0, "A", first)
    start(0, "A")
    finish(1, "K")
    prepare(1)
    gather_finish("K", 0)
    gather_start("K", 1)
    finish(0, "A")
    sweep(0, "A", "B")
    start(0, "B")
    gather_finish("K", 1)
    gather_start("K", 2)
    finish(0, "B")
    restrict(0, residual(0, "B"), 0.5, source(1))
    g1 = ref["g1"]
    fill(1, "A", lambda i: g1[i])
    start(1, "A")

    gather_finish("K", 2)
    v2k = ref["v2K"]

    def store_k(i, row, rows):
        v2k[i + 1, pl.ds(PAD + row, py), :] = rows

    unpack("K", store_k)
    for level in (2, 3):
        v, y = ref["v%dK" % level], plan.dims[level][1]
        restrict(level, lambda i: v[i + 1, pl.ds(PAD, y), :], 0.125, interior(level + 1, "K"))
    for level in (2, 3, 4):
        prepare(level)

    finish(1, "A")
    sweep(1, "A", "B")
    start(1, "B")
    finish(1, "B")
    own_piece(residual(1, "B"), 0.5, "F")
    for stage in range(3):
        gather_start("F", stage)
        gather_finish("F", stage)

    g2, q2 = ref["g2"], ref["q2"]

    def store_f(i, row, rows):
        g2[i, pl.ds(row, py), :] = q2[i, pl.ds(row, py), :] * rows

    unpack("F", store_f)
    for level in (2, 3):
        g = ref["g%d" % level]
        fill(level, "A", lambda i: g[i])
        sweep(level, "A", "B")
        restrict(level, residual(level, "B"), 0.5, source(level + 1))
    g4 = ref["g4"]
    fill(4, "A", lambda i: g4[i])
    at, other = "A", "B"
    for _ in range(COARSE_SWEEPS - 1):
        sweep(4, at, other)
        at, other = other, at
    coarse = "v4" + at
    for level in (3, 2):
        v, y = ref[coarse], plan.dims[level + 1][1]
        correct(level, lambda i: v[i + 1, pl.ds(PAD, y), :])
        sweep(level, "C", "D")
        sweep(level, "D", "E")
        coarse = "v%dE" % level

    e2 = ref["v2E"]

    def own_e2(i):
        rows = e2[me[0] * px + i + 1, pl.ds(pl.multiple_of(PAD + me[1] * py, 8), py), :]
        return pltpu.roll(rows, lax.rem(LANES - me[2] * pz, LANES), 1)

    correct(1, own_e2)
    start(1, "C")
    finish(1, "C")
    sweep(1, "C", "D")
    start(1, "D")
    finish(1, "D")
    sweep(1, "D", "E")
    e1 = ref["v1E"]
    correct(0, lambda i: e1[i + 1, pl.ds(PAD, y1), :])
    start(0, "C")
    finish(0, "C")
    sweep(0, "C", "D")
    start(0, "D")
    finish(0, "D")
    sweep(0, "D", "E")
    start(0, "E")
    y0 = plan.dims[0][1]
    e0 = ref["v0E"]

    def out(i):
        sol_ref[i] = e0[i + 1, pl.ds(PAD, y0), :]

    loop(plan.dims[0][0], out)
    finish(0, "E")
    rest = residual(0, "E")

    def last(i):
        res_ref[i] = rest(i)

    loop(plan.dims[0][0], last)

    for level, field in plan.exchanges:
        drain(level, field)
    for field in "KF":
        for stage in range(3):
            gather_drain(field, stage)


def solution(mesh):
    sizes = tuple(mesh.shape[a] for a in AXES)
    spec = P(*AXES)

    def body(right_side, coefficient):
        plan = Plan(sizes, right_side.shape)
        block = jax.ShapeDtypeStruct(right_side.shape, F32)
        vmem = pl.BlockSpec(memory_space=pltpu.VMEM)
        return pl.pallas_call(
            functools.partial(kernel, plan),
            out_shape=(block, block),
            in_specs=[vmem, vmem],
            out_specs=(vmem, vmem),
            scratch_shapes=plan.shapes,
            compiler_params=pltpu.CompilerParams(
                collective_id=0, has_side_effects=True, vmem_limit_bytes=48 * 2**20),
        )(right_side, coefficient)

    return jax.shard_map(body, mesh=mesh, in_specs=(spec, spec), out_specs=(spec, spec), check_vma=False)
```

```python
import functools
import jax
import jax.numpy as jnp
from jax import lax
from jax.experimental import pallas as pl
from jax.experimental.pallas import tpu as pltpu
from jax.sharding import PartitionSpec as P

NU = 2
COARSE_SWEEPS = 8
OMEGA = 0.8
LANES = 128
PAD = 8
AXES = ("dom", "gy", "gz")
MESH = pl.DeviceIdType.MESH
F32 = jnp.float32
HI = lax.Precision.HIGHEST
UNROLL = 16


def loop(n, body, init=None, unroll=UNROLL):
    unroll = min(unroll, n)
    if init is None:
        lax.fori_loop(0, n, lambda i, c: (body(i), c)[1], 0, unroll=unroll)
        return None
    return lax.fori_loop(0, n, body, init, unroll=unroll)


def lane_index(rows):
    return lax.broadcasted_iota(jnp.int32, (rows, LANES), 1)


def pair_sum_matrix(nz):
    row = lax.broadcasted_iota(jnp.int32, (LANES, LANES), 0)
    col = lax.broadcasted_iota(jnp.int32, (LANES, LANES), 1)
    return jnp.where((row // 2 == col) & (row < nz), 1.0, 0.0).astype(F32)


def pair_copy_matrix(nz):
    row = lax.broadcasted_iota(jnp.int32, (LANES, LANES), 0)
    col = lax.broadcasted_iota(jnp.int32, (LANES, LANES), 1)
    return jnp.where((col // 2 == row) & (col < nz), 1.0, 0.0).astype(F32)


class Plan:
    def __init__(self, sizes, local):
        self.sizes = sizes
        self.names = []
        self.shapes = []
        nx, ny, nz = local
        self.local = local
        self.dims = {0: (nx, ny, nz), 1: (nx // 2, ny // 2, nz // 2)}
        self.piece = (nx // 4, ny // 4, nz // 4)
        for level in (2, 3, 4):
            s = 2**level
            self.dims[level] = tuple(d * n // s for d, n in zip(sizes, local))
        assert self.dims[2][2] <= LANES and self.piece[0] * self.piece[2] <= LANES
        self.rounds = 0
        for level in range(5):
            x, y, z = self.dims[level]
            fields = {0: "KABCDE", 1: "KABCDE", 2: "KABCDE", 3: "KABCDE", 4: "KAB"}[level]
            for field in fields:
                self.add("v%d%s" % (level, field), (x + 2, y + 2 * PAD, LANES))
            self.add("w%d" % level, (6, x, y, LANES))
            for field in "dqg":
                self.add("%s%d" % (field, level), (x, y, LANES))
            if level < 4:
                self.add("t%d" % level, (x // 2, y, LANES))
            if level < 2:
                for field in "KABCDE":
                    self.add("zs%d%s" % (level, field), (2, y, LANES))
                    self.add("zr%d%s" % (level, field), (2, y, LANES))
        for field in "KF":
            self.add("gb" + field, tuple(sizes) + (self.piece[1], LANES))
        self.sem_base = len(self.shapes)
        self.exchanges = {(l, c): i for i, (l, c) in enumerate(
            [(0, "K"), (1, "K"), (0, "A"), (0, "B"), (1, "A"), (1, "B"),
             (1, "C"), (1, "D"), (0, "C"), (0, "D"), (0, "E")])}
        n = len(self.exchanges)
        peers = max(sizes[0] * sizes[1], sizes[2])
        self.names += ["es", "er", "gs", "gr"]
        self.shapes += [pltpu.SemaphoreType.DMA((n, 6)), pltpu.SemaphoreType.DMA((n, 6)),
                        pltpu.SemaphoreType.DMA((4, peers)), pltpu.SemaphoreType.DMA((4, peers))]

    def add(self, name, shape):
        self.names.append(name)
        self.shapes.append(pltpu.VMEM(shape, F32))


def kernel(plan, f_ref, k_ref, sol_ref, res_ref, *scratch):
    ref = dict(zip(plan.names, scratch))
    sizes = plan.sizes
    me = [lax.axis_index(a) for a in AXES]

    def copies(level, field):
        x, y, z = plan.dims[level]
        v = ref["v%d%s" % (level, field)]
        zs, zr = ref["zs%d%s" % (level, field)], ref["zr%d%s" % (level, field)]
        rnd = plan.exchanges[(level, field)]
        rows, planes = pl.ds(PAD, y), pl.ds(1, x)
        ends = [
            (v.at[x, rows], v.at[0, rows]), (v.at[1, rows], v.at[x + 1, rows]),
            (v.at[planes, pl.ds(PAD + y - 1, 1)], v.at[planes, pl.ds(PAD - 1, 1)]),
            (v.at[planes, pl.ds(PAD, 1)], v.at[planes, pl.ds(PAD + y, 1)]),
            (zs.at[1], zr.at[0]), (zs.at[0], zr.at[1]),
        ]
        result = []
        for i, (src, dst) in enumerate(ends):
            axis, up = i // 2, i % 2 == 0
            n, at = sizes[axis], me[axis]
            to = lax.rem(at + 1, n) if up else lax.rem(at + n - 1, n)
            copy = pltpu.make_async_remote_copy(
                src_ref=src, dst_ref=dst, send_sem=ref["es"].at[rnd, i], recv_sem=ref["er"].at[rnd, i],
                device_id={AXES[axis]: to}, device_id_type=MESH)
            sends = at < n - 1 if up else at > 0
            gets = at > 0 if up else at < n - 1
            result.append((copy, sends, gets))
        return result

    def start(level, field):
        for copy, sends, _ in copies(level, field):
            pl.when(sends)(copy.start)

    def finish(level, field):
        for copy, _, gets in copies(level, field):
            pl.when(gets)(copy.wait_recv)

    def drain(level, field):
        for copy, sends, _ in copies(level, field):
            pl.when(sends)(copy.wait_send)

    def zero_edges(level, field):
        x, y, z = plan.dims[level]
        v = ref["v%d%s" % (level, field)]
        zr = ref["zr%d%s" % (level, field)]
        spots = [v.at[0], v.at[x + 1], v.at[pl.ds(0, x + 2), pl.ds(0, PAD)],
                 v.at[pl.ds(0, x + 2), pl.ds(PAD + y, PAD)], zr.at[0], zr.at[1]]
        for i, spot in enumerate(spots):
            edge = me[i // 2] == (0 if i % 2 == 0 else sizes[i // 2] - 1)

            @pl.when(edge)
            def _():
                spot[...] = jnp.zeros(spot.shape, F32)

    def gather_copies(field, stage):
        gb = ref["gb" + field]
        base = (0 if field == "K" else 2) + stage
        x, y, z = sizes
        if stage == 0:
            shifts = [(0, 0, s) for s in range(1, z)]
        else:
            shifts = [(s, t, 0) for s in range(x) for t in range(y) if s or t]
        result = []
        for j, shift in enumerate(shifts):
            to = [lax.rem(at + s, n) for at, s, n in zip(me, shift, sizes)]
            frm = [lax.rem(at + n - s, n) for at, s, n in zip(me, shift, sizes)]
            depth = 3 - stage
            make = functools.partial(
                pltpu.make_async_remote_copy, send_sem=ref["gs"].at[base, j], recv_sem=ref["gr"].at[base, j],
                device_id=tuple(to), device_id_type=MESH)
            index, other = tuple(me[:depth]), tuple(frm[:depth])
            result.append((make(src_ref=gb.at[index], dst_ref=gb.at[index]),
                           make(src_ref=gb.at[other], dst_ref=gb.at[other])))
        return result

    def gather_start(field, stage):
        for out, _ in gather_copies(field, stage):
            out.start()

    def gather_finish(field, stage):
        for _, into in gather_copies(field, stage):
            into.wait_recv()

    def gather_drain(field, stage):
        for out, _ in gather_copies(field, stage):
            out.wait_send()

    def shifted(level, field, i):
        x, y, z = plan.dims[level]
        v = ref["v%d%s" % (level, field)]
        lane = lane_index(y)
        mid = v[i + 1, pl.ds(PAD, y), :]
        zp = pltpu.roll(mid, LANES - 1, 1)
        zm = pltpu.roll(mid, 1, 1)
        if level < 2:
            zr = ref["zr%d%s" % (level, field)]
            zp = jnp.where(lane == z - 1, pltpu.roll(zr[1], lax.rem(LANES + z - 1 - i, LANES), 1), zp)
            zm = jnp.where(lane == 0, pltpu.roll(zr[0], lax.rem(LANES - i, LANES), 1), zm)
        return mid, (v[i + 2, pl.ds(PAD, y), :], v[i, pl.ds(PAD, y), :],
                     v[i + 1, pl.ds(PAD + 1, y), :], v[i + 1, pl.ds(PAD - 1, y), :], zp, zm)

    def total(level, field, i):
        w = ref["w%d" % level]
        mid, beside = shifted(level, field, i)
        parts = [w[j, i] * b for j, b in enumerate(beside)]
        g = ref["g%d" % level][i]
        return mid, ((parts[0] + parts[1]) + (parts[2] + parts[3])) + ((parts[4] + parts[5]) + g)

    def fill(level, field, plane):
        x, y, z = plan.dims[level]
        v = ref["v%d%s" % (level, field)]
        if level < 2 and (level, field) in plan.exchanges:
            lane = lane_index(y)

            def body(i, carry):
                low, high = carry
                value = plane(i)
                v[i + 1, pl.ds(PAD, y), :] = value
                low = jnp.where(lane == i, jnp.broadcast_to(value[:, 0:1], (y, LANES)), low)
                high = jnp.where(lane == i, jnp.broadcast_to(value[:, z - 1:z], (y, LANES)), high)
                return low, high

            zero = jnp.zeros((y, LANES), F32)
            low, high = loop(x, body, (zero, zero))
            zs = ref["zs%d%s" % (level, field)]
            zs[0] = low
            zs[1] = high
        else:
            def body(i):
                v[i + 1, pl.ds(PAD, y), :] = plane(i)

            loop(x, body)

    def sweep(level, src, dst):
        def plane(i):
            mid, t = total(level, src, i)
            return (1.0 - OMEGA) * mid + t

        fill(level, dst, plane)

    def prepare(level):
        x, y, z = plan.dims[level]
        lane = lane_index(y)
        inside = lane < z
        w, d, q = ref["w%d" % level], ref["d%d" % level], ref["q%d" % level]

        def body(i):
            mid, beside = shifted(level, "K", i)
            beside = list(beside)
            if level >= 2:
                beside[4] = jnp.where(lane == z - 1, 0.0, beside[4])
                beside[5] = jnp.where(lane == 0, 0.0, beside[5])
            faces = [0.5 * (mid + b) for b in beside]
            diag = ((faces[0] + faces[1]) + (faces[2] + faces[3])) + (faces[4] + faces[5])
            scale = jnp.where(inside, OMEGA / jnp.where(inside, diag, 1.0), 0.0)
            d[i] = diag * (1.0 / OMEGA)
            q[i] = scale
            for j, face in enumerate(faces):
                weight = face * scale
                if level >= 2 and j == 4:
                    weight = jnp.where(lane == z - 1, 0.0, weight)
                if level >= 2 and j == 5:
                    weight = jnp.where(lane == 0, 0.0, weight)
                w[j, i] = weight

        loop(x, body)

    def restrict(level, plane, factor, store):
        x, y, z = plan.dims[level]
        t = ref["t%d" % level]
        matrix = pair_sum_matrix(z)

        def body(i):
            t[i] = plane(2 * i) + plane(2 * i + 1)

        loop(x // 2, body)

        def second(i):
            rows = t[i, pl.ds(0, y // 2, stride=2), :] + t[i, pl.ds(1, y // 2, stride=2), :]
            store(i, jnp.dot(rows * factor, matrix, precision=HI, preferred_element_type=F32))

        loop(x // 2, second)

    def residual(level, field):
        d = ref["d%d" % level]

        def plane(i):
            mid, t = total(level, field, i)
            return d[i] * (t - OMEGA * mid)

        return plane

    def correct(level, coarse):
        x, y, z = plan.dims[level]
        t = ref["t%d" % level]
        matrix = pair_copy_matrix(z)

        def body(i):
            rows = jnp.dot(coarse(i), matrix, precision=HI, preferred_element_type=F32)
            t[i, pl.ds(0, y // 2, stride=2), :] = rows
            t[i, pl.ds(1, y // 2, stride=2), :] = rows

        loop(x // 2, body)
        vb = ref["v%dB" % level]
        fill(level, "C", lambda i: vb[i + 1, pl.ds(PAD, y), :] + t[i // 2])

    px, py, pz = plan.piece

    def pack(pieces):
        whole = pieces[0]
        for i in range(1, px):
            whole = whole + pltpu.roll(pieces[i], i * pz, 1)
        return whole

    def unpack(field, store):
        gb = ref["gb" + field]
        lane = lane_index(py)
        for a in range(sizes[0]):
            for b in range(sizes[1]):
                for i in range(px):
                    rows = jnp.zeros((py, LANES), F32)
                    for c in range(sizes[2]):
                        part = gb[a, b, c]
                        shift = (pz * (c - i)) % LANES
                        if shift:
                            part = pltpu.roll(part, shift, 1)
                        rows = jnp.where(lane // pz == c, part, rows)
                    store(a * px + i, b * py, rows)

    def interior(level, field):
        x, y, z = plan.dims[level]
        v = ref["v%d%s" % (level, field)]

        def store(i, rows):
            v[i + 1, pl.ds(PAD, y), :] = rows

        return store

    def source(level):
        x, y, z = plan.dims[level]
        g, q = ref["g%d" % level], ref["q%d" % level]

        def store(i, rows):
            g[i] = q[i] * rows

        return store

    for level, field in plan.exchanges:
        zero_edges(level, field)
    barrier = pltpu.get_barrier_semaphore()
    greeted = [(a, b, 0) for a in range(sizes[0]) for b in range(sizes[1]) if a or b]
    greeted += [(0, 0, c) for c in range(1, sizes[2])]
    for shift in greeted:
        to = tuple(lax.rem(at + s, n) for at, s, n in zip(me, shift, sizes))
        pl.semaphore_signal(barrier, inc=1, device_id=to, device_id_type=MESH)

    k_plane = lambda i: k_ref[i]
    fill(0, "K", k_plane)
    restrict(0, k_plane, 0.125, interior(1, "K"))
    k1 = ref["v1K"]
    y1 = plan.dims[1][1]
    k1_plane = lambda i: k1[i + 1, pl.ds(PAD, y1), :]
    fill(1, "K", k1_plane)

    pl.semaphore_wait(barrier, len(greeted))
    start(0, "K")
    start(1, "K")

    def own_piece(level_plane, factor, field):
        t = ref["t0"]

        def store(i, rows):
            t[i, pl.ds(0, py), :] = rows

        restrict(1, level_plane, factor, store)
        ref["gb" + field][me[0], me[1], me[2]] = pack([t[i, pl.ds(0, py), :] for i in range(px)])

    own_piece(k1_plane, 0.125, "K")
    gather_start("K", 0)
    for level in (2, 3, 4):
        x, y, z = plan.dims[level]
        for field in ("KAB" if level == 4 else "KABCDE"):
            v = ref["v%d%s" % (level, field)]
            v[0] = jnp.zeros(v.shape[1:], F32)
            v[x + 1] = jnp.zeros(v.shape[1:], F32)
            v[:, pl.ds(0, PAD), :] = jnp.zeros((x + 2, PAD, LANES), F32)
            v[:, pl.ds(PAD + y, PAD), :] = jnp.zeros((x + 2, PAD, LANES), F32)

    finish(0, "K")
    prepare(0)
    g0, q0 = ref["g0"], ref["q0"]

    def first(i):
        value = q0[i] * f_ref[i]
        g0[i] = value
        return value

    fill(0, "A", first)
    start(0, "A")
    finish(1, "K")
    prepare(1)
    gather_finish("K", 0)
    gather_start("K", 1)
    finish(0, "A")
    sweep(0, "A", "B")
    start(0, "B")
    finish(0, "B")
    restrict(0, residual(0, "B"), 0.5, source(1))
    g1 = ref["g1"]
    fill(1, "A", lambda i: g1[i])
    start(1, "A")

    gather_finish("K", 1)
    v2k = ref["v2K"]

    def store_k(i, row, rows):
        v2k[i + 1, pl.ds(PAD + row, py), :] = rows

    unpack("K", store_k)
    for level in (2, 3):
        v, y = ref["v%dK" % level], plan.dims[level][1]
        restrict(level, lambda i: v[i + 1, pl.ds(PAD, y), :], 0.125, interior(level + 1, "K"))
    for level in (2, 3, 4):
        prepare(level)

    finish(1, "A")
    sweep(1, "A", "B")
    start(1, "B")
    finish(1, "B")
    own_piece(residual(1, "B"), 0.5, "F")
    for stage in range(2):
        gather_start("F", stage)
        gather_finish("F", stage)

    g2, q2 = ref["g2"], ref["q2"]

    def store_f(i, row, rows):
        g2[i, pl.ds(row, py), :] = q2[i, pl.ds(row, py), :] * rows

    unpack("F", store_f)
    for level in (2, 3):
        g = ref["g%d" % level]
        fill(level, "A", lambda i: g[i])
        sweep(level, "A", "B")
        restrict(level, residual(level, "B"), 0.5, source(level + 1))
    g4 = ref["g4"]
    fill(4, "A", lambda i: g4[i])
    at, other = "A", "B"
    for _ in range(COARSE_SWEEPS - 1):
        sweep(4, at, other)
        at, other = other, at
    coarse = "v4" + at
    for level in (3, 2):
        v, y = ref[coarse], plan.dims[level + 1][1]
        correct(level, lambda i: v[i + 1, pl.ds(PAD, y), :])
        sweep(level, "C", "D")
        sweep(level, "D", "E")
        coarse = "v%dE" % level

    e2 = ref["v2E"]

    def own_e2(i):
        rows = e2[me[0] * px + i + 1, pl.ds(pl.multiple_of(PAD + me[1] * py, 8), py), :]
        return pltpu.roll(rows, lax.rem(LANES - me[2] * pz, LANES), 1)

    correct(1, own_e2)
    start(1, "C")
    finish(1, "C")
    sweep(1, "C", "D")
    start(1, "D")
    finish(1, "D")
    sweep(1, "D", "E")
    e1 = ref["v1E"]
    correct(0, lambda i: e1[i + 1, pl.ds(PAD, y1), :])
    start(0, "C")
    finish(0, "C")
    sweep(0, "C", "D")
    start(0, "D")
    finish(0, "D")
    sweep(0, "D", "E")
    start(0, "E")
    y0 = plan.dims[0][1]
    e0 = ref["v0E"]

    def out(i):
        sol_ref[i] = e0[i + 1, pl.ds(PAD, y0), :]

    loop(plan.dims[0][0], out)
    finish(0, "E")
    rest = residual(0, "E")

    def last(i):
        res_ref[i] = rest(i)

    loop(plan.dims[0][0], last)

    for level, field in plan.exchanges:
        drain(level, field)
    for field in "KF":
        for stage in range(2):
            gather_drain(field, stage)


def solution(mesh):
    sizes = tuple(mesh.shape[a] for a in AXES)
    spec = P(*AXES)

    def body(right_side, coefficient):
        plan = Plan(sizes, right_side.shape)
        block = jax.ShapeDtypeStruct(right_side.shape, F32)
        vmem = pl.BlockSpec(memory_space=pltpu.VMEM)
        return pl.pallas_call(
            functools.partial(kernel, plan),
            out_shape=(block, block),
            in_specs=[vmem, vmem],
            out_specs=(vmem, vmem),
            scratch_shapes=plan.shapes,
            compiler_params=pltpu.CompilerParams(
                collective_id=0, has_side_effects=True, vmem_limit_bytes=48 * 2**20),
        )(right_side, coefficient)

    return jax.shard_map(body, mesh=mesh, in_specs=(spec, spec), out_specs=(spec, spec), check_vma=False)
```

```python
import functools
import jax
import jax.numpy as jnp
from jax import lax
from jax.experimental import pallas as pl
from jax.experimental.pallas import tpu as pltpu
from jax.sharding import PartitionSpec as P

NU = 2
COARSE_SWEEPS = 8
OMEGA = 0.8
LANES = 128
PAD = 8
AXES = ("dom", "gy", "gz")
MESH = pl.DeviceIdType.MESH
F32 = jnp.float32
HI = lax.Precision.HIGHEST
UNROLL = 16


def loop(n, body, init=None, unroll=UNROLL):
    unroll = min(unroll, n)
    if init is None:
        lax.fori_loop(0, n, lambda i, c: (body(i), c)[1], 0, unroll=unroll)
        return None
    return lax.fori_loop(0, n, body, init, unroll=unroll)


def lane_index(rows):
    return lax.broadcasted_iota(jnp.int32, (rows, LANES), 1)


def pair_sum_matrix(nz):
    row = lax.broadcasted_iota(jnp.int32, (LANES, LANES), 0)
    col = lax.broadcasted_iota(jnp.int32, (LANES, LANES), 1)
    return jnp.where((row // 2 == col) & (row < nz), 1.0, 0.0).astype(F32)


def pair_copy_matrix(nz):
    row = lax.broadcasted_iota(jnp.int32, (LANES, LANES), 0)
    col = lax.broadcasted_iota(jnp.int32, (LANES, LANES), 1)
    return jnp.where((col // 2 == row) & (col < nz), 1.0, 0.0).astype(F32)


class Plan:
    def __init__(self, sizes, local):
        self.sizes = sizes
        self.names = []
        self.shapes = []
        nx, ny, nz = local
        self.local = local
        self.dims = {0: (nx, ny, nz), 1: (nx // 2, ny // 2, nz // 2)}
        self.piece = (nx // 4, ny // 4, nz // 4)
        for level in (2, 3, 4):
            s = 2**level
            self.dims[level] = tuple(d * n // s for d, n in zip(sizes, local))
        assert self.dims[2][2] <= LANES and self.piece[0] * self.piece[2] <= LANES
        self.rounds = 0
        for level in range(5):
            x, y, z = self.dims[level]
            fields = {0: "KABCDE", 1: "KABCDE", 2: "KABCDE", 3: "KABCDE", 4: "KAB"}[level]
            for field in fields:
                self.add("v%d%s" % (level, field), (x + 2, y + 2 * PAD, LANES))
            self.add("w%d" % level, (6, x, y, LANES))
            for field in "dqg":
                self.add("%s%d" % (field, level), (x, y, LANES))
            if level < 4:
                self.add("t%d" % level, (x // 2, y, LANES))
            if level < 2:
                for field in "KABCDE":
                    self.add("zs%d%s" % (level, field), (2, PAD, LANES))
                    self.add("zr%d%s" % (level, field), (2, PAD, LANES))
                self.add("zx%d" % level, (2, y, LANES))
                assert y % PAD == 0 and x * (y // PAD) <= LANES
        for field in "KF":
            self.add("gb" + field, tuple(sizes) + (self.piece[1], LANES))
        self.sem_base = len(self.shapes)
        self.exchanges = {(l, c): i for i, (l, c) in enumerate(
            [(0, "K"), (1, "K"), (0, "A"), (0, "B"), (1, "A"), (1, "B"),
             (1, "D"), (0, "C"), (0, "D"), (0, "E")])}
        n = len(self.exchanges)
        peers = max(sizes[0] * sizes[1], sizes[2])
        self.names += ["es", "er", "gs", "gr"]
        self.shapes += [pltpu.SemaphoreType.DMA((n, 6)), pltpu.SemaphoreType.DMA((n, 6)),
                        pltpu.SemaphoreType.DMA((4, peers)), pltpu.SemaphoreType.DMA((4, peers))]

    def add(self, name, shape):
        self.names.append(name)
        self.shapes.append(pltpu.VMEM(shape, F32))


def kernel(plan, f_ref, k_ref, sol_ref, res_ref, *scratch):
    ref = dict(zip(plan.names, scratch))
    sizes = plan.sizes
    me = [lax.axis_index(a) for a in AXES]

    def copies(level, field):
        x, y, z = plan.dims[level]
        v = ref["v%d%s" % (level, field)]
        zs, zr = ref["zs%d%s" % (level, field)], ref["zr%d%s" % (level, field)]
        rnd = plan.exchanges[(level, field)]
        rows, planes = pl.ds(PAD, y), pl.ds(1, x)
        ends = [
            (v.at[x, rows], v.at[0, rows]), (v.at[1, rows], v.at[x + 1, rows]),
            (v.at[planes, pl.ds(PAD + y - 1, 1)], v.at[planes, pl.ds(PAD - 1, 1)]),
            (v.at[planes, pl.ds(PAD, 1)], v.at[planes, pl.ds(PAD + y, 1)]),
            (zs.at[1], zr.at[0]), (zs.at[0], zr.at[1]),
        ]
        result = []
        for i, (src, dst) in enumerate(ends):
            axis, up = i // 2, i % 2 == 0
            n, at = sizes[axis], me[axis]
            to = lax.rem(at + 1, n) if up else lax.rem(at + n - 1, n)
            copy = pltpu.make_async_remote_copy(
                src_ref=src, dst_ref=dst, send_sem=ref["es"].at[rnd, i], recv_sem=ref["er"].at[rnd, i],
                device_id={AXES[axis]: to}, device_id_type=MESH)
            sends = at < n - 1 if up else at > 0
            gets = at > 0 if up else at < n - 1
            result.append((copy, sends, gets))
        return result

    def start(level, field):
        made = copies(level, field)
        for copy, sends, _ in made[4:] + made[:4]:
            pl.when(sends)(copy.start)

    def finish(level, field):
        for copy, _, gets in copies(level, field):
            pl.when(gets)(copy.wait_recv)
        x, y, z = plan.dims[level]
        zr, zx = ref["zr%d%s" % (level, field)], ref["zx%d" % level]
        for side in range(2):
            face = zr[side]
            for g in range(y // PAD):
                zx[side, pl.ds(PAD * g, PAD), :] = pltpu.roll(face, LANES - x * g, 1) if g else face

    def drain(level, field):
        for copy, sends, _ in copies(level, field):
            pl.when(sends)(copy.wait_send)

    def zero_edges(level, field):
        x, y, z = plan.dims[level]
        v = ref["v%d%s" % (level, field)]
        zr = ref["zr%d%s" % (level, field)]
        spots = [v.at[0], v.at[x + 1], v.at[pl.ds(0, x + 2), pl.ds(0, PAD)],
                 v.at[pl.ds(0, x + 2), pl.ds(PAD + y, PAD)], zr.at[0], zr.at[1]]
        for i, spot in enumerate(spots):
            edge = me[i // 2] == (0 if i % 2 == 0 else sizes[i // 2] - 1)

            @pl.when(edge)
            def _():
                spot[...] = jnp.zeros(spot.shape, F32)

    def gather_copies(field, stage):
        gb = ref["gb" + field]
        base = (0 if field == "K" else 2) + stage
        x, y, z = sizes
        if stage == 0:
            shifts = [(0, 0, s) for s in range(1, z)]
        else:
            shifts = [(s, t, 0) for s in range(x) for t in range(y) if s or t]
        result = []
        for j, shift in enumerate(shifts):
            to = [lax.rem(at + s, n) for at, s, n in zip(me, shift, sizes)]
            frm = [lax.rem(at + n - s, n) for at, s, n in zip(me, shift, sizes)]
            depth = 3 - stage
            make = functools.partial(
                pltpu.make_async_remote_copy, send_sem=ref["gs"].at[base, j], recv_sem=ref["gr"].at[base, j],
                device_id=tuple(to), device_id_type=MESH)
            index, other = tuple(me[:depth]), tuple(frm[:depth])
            result.append((make(src_ref=gb.at[index], dst_ref=gb.at[index]),
                           make(src_ref=gb.at[other], dst_ref=gb.at[other])))
        return result

    def gather_start(field, stage):
        for out, _ in gather_copies(field, stage):
            out.start()

    def gather_finish(field, stage):
        for _, into in gather_copies(field, stage):
            into.wait_recv()

    def gather_drain(field, stage):
        for out, _ in gather_copies(field, stage):
            out.wait_send()

    def shifted(level, field, i):
        x, y, z = plan.dims[level]
        v = ref["v%d%s" % (level, field)]
        lane = lane_index(y)
        mid = v[i + 1, pl.ds(PAD, y), :]
        zp = pltpu.roll(mid, LANES - 1, 1)
        zm = pltpu.roll(mid, 1, 1)
        if level < 2:
            zr = ref["zx%d" % level]
            zp = jnp.where(lane == z - 1, pltpu.roll(zr[1], lax.rem(LANES + z - 1 - i, LANES), 1), zp)
            zm = jnp.where(lane == 0, pltpu.roll(zr[0], lax.rem(LANES - i, LANES), 1), zm)
        return mid, (v[i + 2, pl.ds(PAD, y), :], v[i, pl.ds(PAD, y), :],
                     v[i + 1, pl.ds(PAD + 1, y), :], v[i + 1, pl.ds(PAD - 1, y), :], zp, zm)

    def total(level, field, i):
        w = ref["w%d" % level]
        mid, beside = shifted(level, field, i)
        parts = [w[j, i] * b for j, b in enumerate(beside)]
        g = ref["g%d" % level][i]
        return mid, ((parts[0] + parts[1]) + (parts[2] + parts[3])) + ((parts[4] + parts[5]) + g)

    def fill(level, field, plane):
        x, y, z = plan.dims[level]
        v = ref["v%d%s" % (level, field)]
        if level < 2 and (level, field) in plan.exchanges:
            lane = lane_index(y)

            def body(i, carry):
                low, high = carry
                value = plane(i)
                v[i + 1, pl.ds(PAD, y), :] = value
                low = jnp.where(lane == i, jnp.broadcast_to(value[:, 0:1], (y, LANES)), low)
                high = jnp.where(lane == i, jnp.broadcast_to(value[:, z - 1:z], (y, LANES)), high)
                return low, high

            zero = jnp.zeros((y, LANES), F32)
            low, high = loop(x, body, (zero, zero))
            zs = ref["zs%d%s" % (level, field)]
            for side, face in enumerate((low, high)):
                parts = [face[PAD * g:PAD * (g + 1)] for g in range(y // PAD)]
                parts = [pltpu.roll(p, x * g, 1) if g else p for g, p in enumerate(parts)]
                while len(parts) > 1:
                    parts = [sum(parts[k + 1:k + 2], parts[k]) for k in range(0, len(parts), 2)]
                zs[side] = parts[0]
        else:
            def body(i):
                v[i + 1, pl.ds(PAD, y), :] = plane(i)

            loop(x, body)

    def sweep(level, src, dst):
        def plane(i):
            mid, t = total(level, src, i)
            return (1.0 - OMEGA) * mid + t

        fill(level, dst, plane)

    def prepare(level):
        x, y, z = plan.dims[level]
        lane = lane_index(y)
        inside = lane < z
        w, d, q = ref["w%d" % level], ref["d%d" % level], ref["q%d" % level]

        def body(i):
            mid, beside = shifted(level, "K", i)
            beside = list(beside)
            if level >= 2:
                beside[4] = jnp.where(lane == z - 1, 0.0, beside[4])
                beside[5] = jnp.where(lane == 0, 0.0, beside[5])
            faces = [0.5 * (mid + b) for b in beside]
            diag = ((faces[0] + faces[1]) + (faces[2] + faces[3])) + (faces[4] + faces[5])
            scale = jnp.where(inside, OMEGA / jnp.where(inside, diag, 1.0), 0.0)
            d[i] = diag * (1.0 / OMEGA)
            q[i] = scale
            for j, face in enumerate(faces):
                weight = face * scale
                if level >= 2 and j == 4:
                    weight = jnp.where(lane == z - 1, 0.0, weight)
                if level >= 2 and j == 5:
                    weight = jnp.where(lane == 0, 0.0, weight)
                w[j, i] = weight

        loop(x, body)

    def restrict(level, plane, factor, store):
        x, y, z = plan.dims[level]
        t = ref["t%d" % level]
        matrix = pair_sum_matrix(z)

        def body(i):
            t[i] = plane(2 * i) + plane(2 * i + 1)

        loop(x // 2, body)

        def second(i):
            rows = t[i, pl.ds(0, y // 2, stride=2), :] + t[i, pl.ds(1, y // 2, stride=2), :]
            store(i, jnp.dot(rows * factor, matrix, precision=HI, preferred_element_type=F32))

        loop(x // 2, second)

    def residual(level, field):
        d = ref["d%d" % level]

        def plane(i):
            mid, t = total(level, field, i)
            return d[i] * (t - OMEGA * mid)

        return plane

    def correct(level, coarse):
        x, y, z = plan.dims[level]
        t = ref["t%d" % level]
        matrix = pair_copy_matrix(z)

        def body(i):
            rows = jnp.dot(coarse(i), matrix, precision=HI, preferred_element_type=F32)
            t[i, pl.ds(0, y // 2, stride=2), :] = rows
            t[i, pl.ds(1, y // 2, stride=2), :] = rows

        loop(x // 2, body)
        vb = ref["v%dB" % level]
        fill(level, "C", lambda i: vb[i + 1, pl.ds(PAD, y), :] + t[i // 2])

    px, py, pz = plan.piece

    def pack(pieces):
        whole = pieces[0]
        for i in range(1, px):
            whole = whole + pltpu.roll(pieces[i], i * pz, 1)
        return whole

    def unpack(field, store):
        gb = ref["gb" + field]
        lane = lane_index(py)
        for a in range(sizes[0]):
            for b in range(sizes[1]):
                for i in range(px):
                    rows = jnp.zeros((py, LANES), F32)
                    for c in range(sizes[2]):
                        part = gb[a, b, c]
                        shift = (pz * (c - i)) % LANES
                        if shift:
                            part = pltpu.roll(part, shift, 1)
                        rows = jnp.where(lane // pz == c, part, rows)
                    store(a * px + i, b * py, rows)

    def interior(level, field):
        x, y, z = plan.dims[level]
        v = ref["v%d%s" % (level, field)]

        def store(i, rows):
            v[i + 1, pl.ds(PAD, y), :] = rows

        return store

    def source(level):
        x, y, z = plan.dims[level]
        g, q = ref["g%d" % level], ref["q%d" % level]

        def store(i, rows):
            g[i] = q[i] * rows

        return store

    for level, field in plan.exchanges:
        zero_edges(level, field)
    barrier = pltpu.get_barrier_semaphore()
    greeted = [(a, b, 0) for a in range(sizes[0]) for b in range(sizes[1]) if a or b]
    greeted += [(0, 0, c) for c in range(1, sizes[2])]
    for shift in greeted:
        to = tuple(lax.rem(at + s, n) for at, s, n in zip(me, shift, sizes))
        pl.semaphore_signal(barrier, inc=1, device_id=to, device_id_type=MESH)

    k_plane = lambda i: k_ref[i]
    fill(0, "K", k_plane)
    restrict(0, k_plane, 0.125, interior(1, "K"))
    k1 = ref["v1K"]
    y1 = plan.dims[1][1]
    k1_plane = lambda i: k1[i + 1, pl.ds(PAD, y1), :]
    fill(1, "K", k1_plane)

    pl.semaphore_wait(barrier, len(greeted))
    start(0, "K")
    start(1, "K")

    def own_piece(level_plane, factor, field):
        t = ref["t0"]

        def store(i, rows):
            t[i, pl.ds(0, py), :] = rows

        restrict(1, level_plane, factor, store)
        ref["gb" + field][me[0], me[1], me[2]] = pack([t[i, pl.ds(0, py), :] for i in range(px)])

    own_piece(k1_plane, 0.125, "K")
    gather_start("K", 0)
    for level in (2, 3, 4):
        x, y, z = plan.dims[level]
        for field in ("KAB" if level == 4 else "KABCDE"):
            v = ref["v%d%s" % (level, field)]
            v[0] = jnp.zeros(v.shape[1:], F32)
            v[x + 1] = jnp.zeros(v.shape[1:], F32)
            v[:, pl.ds(0, PAD), :] = jnp.zeros((x + 2, PAD, LANES), F32)
            v[:, pl.ds(PAD + y, PAD), :] = jnp.zeros((x + 2, PAD, LANES), F32)

    finish(0, "K")
    prepare(0)
    g0, q0 = ref["g0"], ref["q0"]

    def first(i):
        value = q0[i] * f_ref[i]
        g0[i] = value
        return value

    fill(0, "A", first)
    start(0, "A")
    finish(1, "K")
    prepare(1)
    gather_finish("K", 0)
    gather_start("K", 1)
    finish(0, "A")
    sweep(0, "A", "B")
    start(0, "B")
    finish(0, "B")
    restrict(0, residual(0, "B"), 0.5, source(1))
    g1 = ref["g1"]
    fill(1, "A", lambda i: g1[i])
    start(1, "A")

    gather_finish("K", 1)
    v2k = ref["v2K"]

    def store_k(i, row, rows):
        v2k[i + 1, pl.ds(PAD + row, py), :] = rows

    unpack("K", store_k)
    for level in (2, 3):
        v, y = ref["v%dK" % level], plan.dims[level][1]
        restrict(level, lambda i: v[i + 1, pl.ds(PAD, y), :], 0.125, interior(level + 1, "K"))
    for level in (2, 3, 4):
        prepare(level)

    finish(1, "A")
    sweep(1, "A", "B")
    start(1, "B")
    finish(1, "B")
    own_piece(residual(1, "B"), 0.5, "F")
    for stage in range(2):
        gather_start("F", stage)
        gather_finish("F", stage)

    g2, q2 = ref["g2"], ref["q2"]

    def store_f(i, row, rows):
        g2[i, pl.ds(row, py), :] = q2[i, pl.ds(row, py), :] * rows

    unpack("F", store_f)
    for level in (2, 3):
        g = ref["g%d" % level]
        fill(level, "A", lambda i: g[i])
        sweep(level, "A", "B")
        restrict(level, residual(level, "B"), 0.5, source(level + 1))
    g4 = ref["g4"]
    fill(4, "A", lambda i: g4[i])
    at, other = "A", "B"
    for _ in range(COARSE_SWEEPS - 1):
        sweep(4, at, other)
        at, other = other, at
    coarse = "v4" + at
    for level in (3, 2):
        v, y = ref[coarse], plan.dims[level + 1][1]
        correct(level, lambda i: v[i + 1, pl.ds(PAD, y), :])
        sweep(level, "C", "D")
        sweep(level, "D", "E")
        coarse = "v%dE" % level

    e2 = ref["v2E"]

    def own_e2(i):
        rows = e2[me[0] * px + i + 1, pl.ds(pl.multiple_of(PAD + me[1] * py, 8), py), :]
        return pltpu.roll(rows, lax.rem(LANES - me[2] * pz, LANES), 1)

    correct(1, own_e2)

    x1, z1 = plan.dims[1][0], plan.dims[1][2]
    vb, vc, t, zx = ref["v1B"], ref["v1C"], ref["t1"], ref["zx1"]
    matrix = pair_copy_matrix(z1)
    spread = lambda rows: jnp.dot(rows, matrix, precision=HI, preferred_element_type=F32)
    inner = pl.ds(PAD, y1)
    for j, (coarse_x, fine_x) in enumerate(((-1, 0), (px, x1 + 1))):
        rows = spread(own_e2(coarse_x))
        t[j, pl.ds(0, py, stride=2), :] = rows
        t[j, pl.ds(1, py, stride=2), :] = rows
        vc[fine_x, inner, :] = vb[fine_x, inner, :] + t[j]
    shift_z = lax.rem(LANES - me[2] * pz, LANES)
    lane = lane_index(py)
    low, high = jnp.zeros((py, LANES), F32), jnp.zeros((py, LANES), F32)
    for i in range(px):
        for first_row, row, fine_y in ((0, PAD - 1, PAD - 1), (PAD + py, 0, PAD + y1)):
            start_row = pl.multiple_of(me[1] * py + first_row, 8)
            rows = e2[me[0] * px + i + 1, pl.ds(start_row, PAD), :]
            rows = spread(pltpu.roll(rows, shift_z, 1))[row:row + 1]
            for k in (2 * i + 1, 2 * i + 2):
                vc[k, pl.ds(fine_y, 1), :] = vb[k, pl.ds(fine_y, 1), :] + rows
        rows = own_e2(i)
        low = jnp.where(lane // 2 == i, jnp.broadcast_to(rows[:, LANES - 1:], (py, LANES)), low)
        beyond = pz % LANES
        high = jnp.where(lane // 2 == i, jnp.broadcast_to(rows[:, beyond:beyond + 1], (py, LANES)), high)
    low = jnp.where(me[2] > 0, low, 0.0)
    high = jnp.where(me[2] < sizes[2] - 1, high, 0.0)
    for j, rows in enumerate((low, high)):
        t[j, pl.ds(0, py, stride=2), :] = rows
        t[j, pl.ds(1, py, stride=2), :] = rows
        zx[j] = zx[j] + t[j]
    sweep(1, "C", "D")
    start(1, "D")
    finish(1, "D")
    sweep(1, "D", "E")
    e1 = ref["v1E"]
    correct(0, lambda i: e1[i + 1, pl.ds(PAD, y1), :])
    start(0, "C")
    finish(0, "C")
    sweep(0, "C", "D")
    start(0, "D")
    finish(0, "D")
    sweep(0, "D", "E")
    start(0, "E")
    y0 = plan.dims[0][1]
    e0 = ref["v0E"]

    def out(i):
        sol_ref[i] = e0[i + 1, pl.ds(PAD, y0), :]

    loop(plan.dims[0][0], out)
    finish(0, "E")
    rest = residual(0, "E")

    def last(i):
        res_ref[i] = rest(i)

    loop(plan.dims[0][0], last)

    for level, field in plan.exchanges:
        drain(level, field)
    for field in "KF":
        for stage in range(2):
            gather_drain(field, stage)


def solution(mesh):
    sizes = tuple(mesh.shape[a] for a in AXES)
    spec = P(*AXES)

    def body(right_side, coefficient):
        plan = Plan(sizes, right_side.shape)
        block = jax.ShapeDtypeStruct(right_side.shape, F32)
        vmem = pl.BlockSpec(memory_space=pltpu.VMEM)
        return pl.pallas_call(
            functools.partial(kernel, plan),
            out_shape=(block, block),
            in_specs=[vmem, vmem],
            out_specs=(vmem, vmem),
            scratch_shapes=plan.shapes,
            compiler_params=pltpu.CompilerParams(
                collective_id=0, has_side_effects=True, vmem_limit_bytes=48 * 2**20),
        )(right_side, coefficient)

    return jax.shard_map(body, mesh=mesh, in_specs=(spec, spec), out_specs=(spec, spec), check_vma=False)
```
